32 devices in a mesh: req: 4 (over z), cand: 8 (over y, x, core).
Axes of the slice: x: 2, y: 2, z: 4, core: 2. Of those that a mesh axis runs over, the one named last changes fastest.
Arguments:
- dense_feat: bfloat16 [4096, 896], P(('req', 'cand')), may hold values from -6 to 6
- emb_ids: int32 [8, 4, 4096], P('cand', None, 'req'), may hold values from 0 to 32767
- tables: bfloat16 [8, 16, 32768], P('cand'), may hold values from -3 to 3
- history_kv: bfloat16 [8, 64, 2048], P('req', 'cand'), may hold values from -6 to 6
- hist_len: int32 [8], P('req'), may hold values from 1 to 64, 256 in all
- cand_request: int32 [4096], P(('req', 'cand')), may hold values from 0 to 1
- w_query: bfloat16 [1024, 1024], P(('req', 'cand')), may hold values from -0.1875 to 0.1875
- w_out: bfloat16 [1024, 1024], P(('req', 'cand')), may hold values from -0.1875 to 0.1875
- cotangent: bfloat16 [4096, 1024], P(('req', 'cand')), may hold values from -2 to 2
Outputs:
- cand_out: bfloat16 [4096, 1024], P(('req', 'cand'))
- d_kv: float32 [8, 64, 2048], P('req', 'cand')
- d_pooled: bfloat16 [8, 16, 4096], P('cand', None, 'req')
The draws below stay inside these ranges and needn't reach their ends.
Inputs may be any that keep to these rules, and one draw needn't show every extreme that they name: `hist_len`: the lengths sum to 256 and the largest equals 64.
All inputs are finite; a program needn't handle non-finite values. No bound on the sum of `hist_len` on one device may be relied on, other than what follows from the above.
Results may differ from the reference program's by a relative error of at most 0.023.
Values may be sent and summed in bfloat16 or wider, within the bound.
A program may use at most 64 MiB of HBM per device.

```python
import math
import jax
import jax.numpy as jnp
import numpy as np
from jax import lax

D = 1024
H = 8
EMB = 16
TABLES = 8
DENSE = 896
ROWS = 32768
BAG = 4
REQ_OWN = 2
HIST = 64
CAND_DEV = 128
NREQ = 8
CANDS = 4096
N_REQ = 4
N_CAND = 8


def set_ends(result, rng, low, largest):
    spot = [jax.random.randint(jax.random.fold_in(rng, axis), (), 0, length) for axis, length in enumerate(result.shape)]
    main_axis = result.shape.index(max(result.shape))
    next_to = spot[:main_axis] + [(spot[main_axis] + 1) % result.shape[main_axis]] + spot[main_axis + 1:]
    return result.at[tuple(spot)].set(low).at[tuple(next_to)].set(largest)


def levels(rng, shape, cuts, smallest, high):
    loudness = 1.0
    for dim, blocks in cuts:
        steps = jax.random.uniform(jax.random.fold_in(jax.random.fold_in(rng, 6), dim), (blocks,), jnp.float32, smallest / len(cuts), high / len(cuts))
        loudness = loudness * jnp.repeat(jnp.exp(steps), shape[dim] // blocks).reshape((-1,) + (1,) * (len(shape) - 1 - dim))
    return loudness


def rank_bounds(count, lean):
    portions = [(1 << 20) // math.isqrt(grade ** lean) + 1 for grade in range(1, count + 1)]
    scale = 1 + sum(portions) // (1 << 30)
    return np.cumsum(np.array([max(1, weight // scale) for weight in portions]))


def skewed_ids(own_key, extent, number_of, slope):
    grid = rank_bounds(number_of, slope)
    pick = jax.random.randint(jax.random.fold_in(own_key, 1), extent, 0, int(grid[number_of - 1]))
    rank = jnp.searchsorted(jnp.asarray(grid, jnp.int32), pick, side="right")
    return jax.random.permutation(jax.random.fold_in(own_key, 2), number_of)[rank].astype(jnp.int32)


def profile(count, total, reach, skew):
    loads = [(1 << 20) // math.isqrt(rank ** skew) + 1 for rank in range(2, count + 1)]
    rest, counts = total - reach - (count - 1), [1] * (count - 1)
    while rest > 0:
        movable = [i for i in range(count - 1) if counts[i] < reach]
        whole, remaining = sum([loads[i] for i in movable]), rest
        for i in movable:
            more = min(reach - counts[i], max(1, remaining * loads[i] // whole), rest)
            counts[i] = counts[i] + more
            rest = rest - more
    return np.array([reach] + counts)


def ragged(key, count, total, reach, lean):
    if count == 2:
        one = jax.random.randint(key, (), max(1, total - reach), min(reach, total - 1) + 1)
        return jnp.stack([one, total - one])
    sizes = jnp.asarray(profile(count, total, reach, lean), jnp.int32)
    pairs = (count - 1) // 2
    donor, sink = sizes[1:1 + 2 * pairs:2], sizes[2:2 + 2 * pairs:2]
    slack = jnp.minimum(donor - 1, reach - sink)
    shifted = jax.random.randint(jax.random.fold_in(key, 1), (pairs,), 0, 1 << 20) % (slack + 1)
    sizes = sizes.at[1:1 + 2 * pairs:2].set(donor - shifted).at[2:2 + 2 * pairs:2].set(sink + shifted)
    return sizes[jax.random.permutation(jax.random.fold_in(key, 2), count)]


def gaussian(key, shape, spread, most, cuts=(), kind=jnp.bfloat16):
    factor_of = levels(key, shape, cuts, -0.22, 0.18) if cuts else 1.0
    drawn = jax.random.normal(key, shape, jnp.float32) * spread * factor_of
    return jnp.minimum(jnp.maximum(drawn, -most), most).astype(kind)


def setup_inputs(seed: int = 0) -> dict:
    keys = jax.random.split(jax.random.key(seed), 10)
    return {
        "dense_feat": gaussian(keys[0], (CANDS, DENSE), 1.0, 6.0, ((0, 32),)),
        "emb_ids": set_ends(skewed_ids(keys[1], (TABLES, BAG, CANDS), ROWS, 2), jax.random.fold_in(keys[1], 3), 0, ROWS - 1).astype(jnp.int32),
        "tables": gaussian(keys[2], (TABLES, EMB, ROWS), 0.5, 3.0, ((0, 8),)),
        "history_kv": gaussian(keys[3], (NREQ, HIST, 2 * D), 1.0, 6.0, ((0, 4), (1, 8))),
        "hist_len": ragged(keys[4], NREQ, NREQ * HIST // 2, HIST, 2).astype(jnp.int32),
        "cand_request": set_ends(jax.random.randint(keys[5], (CANDS,), 0, REQ_OWN), jax.random.fold_in(keys[5], 1), 0, REQ_OWN - 1).astype(jnp.int32),
        "w_query": gaussian(keys[6], (D, D), D ** -0.5, 0.1875, ((0, 32),)),
        "w_out": gaussian(keys[7], (D, D), D ** -0.5, 0.1875, ((0, 32),)),
        "cotangent": gaussian(keys[8], (CANDS, D), 0.25, 2.0, ((0, 32),)),
    }


norm_eps = 1e-05

def silu_slope(argument):
    sigmoid_value = jax.nn.sigmoid(argument)
    return sigmoid_value * (1.0 + argument * (1.0 - sigmoid_value))

def rounded(argument):
    return lax.optimization_barrier(argument.astype(jnp.bfloat16)).astype(jnp.float32)

def take_columns(table, indices):
    return jnp.take(table, indices, axis=1)

def device_step(features, requests, history, lengths, back_cot, w_query, w_out):
    cand_count, model_width = features.shape
    owned_count, hist_events, kv_width = history.shape
    events = owned_count * hist_events
    head_dim = model_width // H
    score_scale = 1.0 / math.sqrt(head_dim)
    pooled_width = TABLES * EMB
    query_pre = jnp.dot(features, w_query, preferred_element_type=jnp.float32)
    query_heads = rounded(jax.nn.silu(query_pre)).reshape(cand_count, H, head_dim)
    flat_events = history.reshape(events, kv_width).astype(jnp.float32)
    key_heads = flat_events[:, :model_width].reshape(events, H, head_dim)
    value_heads = flat_events[:, model_width:].reshape(events, H, head_dim)
    owner = (jnp.arange(events) // hist_events).astype(jnp.int32)
    position = (jnp.arange(events) % hist_events).astype(jnp.int32)
    in_length = position < lengths[owner]
    live_mask = ((requests[:, None] == owner[None, :]) & in_length[None, :]).astype(jnp.float32)
    scores = jnp.einsum('chd,ehd->che', query_heads, key_heads) * score_scale
    weights = rounded(jax.nn.silu(scores) * live_mask[:, None, :])
    attended = jnp.einsum('che,ehd->chd', weights, value_heads).reshape(cand_count, model_width)
    centered = attended - lax.optimization_barrier(jnp.mean(attended, axis=1, keepdims=True))
    inverse = lax.rsqrt(lax.optimization_barrier(jnp.mean(centered * centered, axis=1, keepdims=True)) + norm_eps)
    normed = centered * inverse
    mixed_out = jnp.dot(normed.astype(jnp.bfloat16), w_out, preferred_element_type=jnp.float32)
    cand_out = (mixed_out + features.astype(jnp.float32)).astype(jnp.bfloat16)
    back_y = jnp.dot(back_cot, w_out.T, preferred_element_type=jnp.float32)
    back_att = inverse * (back_y - lax.optimization_barrier(jnp.mean(back_y, axis=1, keepdims=True)) - normed * lax.optimization_barrier(jnp.mean(back_y * normed, axis=1, keepdims=True)))
    back_att = rounded(back_att).reshape(cand_count, H, head_dim)
    back_w = jnp.einsum('chd,ehd->che', back_att, value_heads)
    back_s = rounded(back_w * live_mask[:, None, :] * silu_slope(scores) * score_scale)
    back_query = jnp.einsum('che,ehd->chd', back_s, key_heads).reshape(cand_count, model_width)
    key_part = jnp.einsum('che,chd->ehd', back_s, query_heads).reshape(events, model_width)
    value_part = jnp.einsum('che,chd->ehd', weights, back_att).reshape(events, model_width)
    kv_part = jnp.concatenate([key_part, value_part], axis=1).astype(jnp.bfloat16)
    back_pre = (back_query * silu_slope(query_pre)).astype(jnp.bfloat16)
    back_pool = back_cot[:, :pooled_width].astype(jnp.float32) + jnp.dot(back_pre, w_query[:pooled_width].T, preferred_element_type=jnp.float32)
    return (cand_out, kv_part.reshape(owned_count, hist_events, kv_width), back_pool.astype(jnp.bfloat16))

def reference(dense_feat, emb_ids, tables, history_kv, hist_len, cand_request, w_query, w_out, cotangent):
    group_size = CAND_DEV * N_CAND

    def one_row(row_index):
        first_cand = (row_index * group_size).astype(jnp.int32)
        first_req = (row_index * REQ_OWN).astype(jnp.int32)
        row_ids = lax.dynamic_slice_in_dim(emb_ids, first_cand, group_size, 2)
        looked_up = jax.vmap(take_columns)(tables, row_ids)
        pooled = lax.optimization_barrier(jnp.sum(looked_up.astype(jnp.float32), axis=2)).astype(jnp.bfloat16)
        pooled = jnp.transpose(pooled, (2, 0, 1)).reshape(group_size, TABLES * EMB)
        features = jnp.concatenate([pooled, lax.dynamic_slice_in_dim(dense_feat, first_cand, group_size, 0)], axis=1)
        history = lax.dynamic_slice_in_dim(history_kv, first_req, REQ_OWN, 0)
        lengths = lax.dynamic_slice_in_dim(hist_len, first_req, REQ_OWN, 0)
        requests = lax.dynamic_slice_in_dim(cand_request, first_cand, group_size, 0)
        back_cot = lax.dynamic_slice_in_dim(cotangent, first_cand, group_size, 0)

        def one_device(device_index):
            first_row = (device_index * CAND_DEV).astype(jnp.int32)
            return device_step(lax.dynamic_slice_in_dim(features, first_row, CAND_DEV, 0), lax.dynamic_slice_in_dim(requests, first_row, CAND_DEV, 0), history, lengths, lax.dynamic_slice_in_dim(back_cot, first_row, CAND_DEV, 0), w_query, w_out)
        row_outputs, kv_parts, pool_grads = lax.map(one_device, jnp.arange(N_CAND, dtype=jnp.int32))
        kv_total = lax.optimization_barrier(jnp.sum(kv_parts.astype(jnp.float32), axis=0))
        return (row_outputs.reshape(group_size, D), kv_total, pool_grads.reshape(group_size, TABLES * EMB))
    row_outputs, kv_grads, pool_grads = lax.map(one_row, jnp.arange(N_REQ, dtype=jnp.int32))
    d_pooled = jnp.transpose(pool_grads.reshape(CANDS, TABLES * EMB), (1, 0)).reshape(TABLES, EMB, CANDS)
    return (row_outputs.reshape(CANDS, D), kv_grads.reshape(NREQ, HIST, 2 * D), d_pooled)
```

```python
import functools
import math

import jax
import jax.numpy as jnp
from jax import lax
from jax.experimental import pallas as pl
from jax.experimental.pallas import tpu as pltpu
from jax.sharding import PartitionSpec as P

H = 8


norm_eps = 1e-05


def silu_slope(argument):
    sigmoid_value = jax.nn.sigmoid(argument)
    return sigmoid_value * (1.0 + argument * (1.0 - sigmoid_value))


def event_mask(requests, lengths, row_count):
    owned_count = lengths.shape[0]
    positions = jnp.arange(row_count, dtype=jnp.int32)
    in_length = positions[None, :] < lengths[:, None]
    same_request = requests[:, None] == jnp.arange(owned_count, dtype=jnp.int32)[None, :]
    joined_mask = same_request[:, :, None] & in_length[None, :, :]
    return joined_mask.reshape(requests.shape[0], owned_count * row_count).astype(jnp.float32)


def forward_events(query_heads, kv_piece, live_mask, score_scale):
    owned_count, row_count, kv_width = kv_piece.shape
    model_width = kv_width // 2
    events = owned_count * row_count
    flat_events = kv_piece.reshape(events, kv_width)
    key_heads = flat_events[:, :model_width].reshape(events, H, model_width // H)
    value_heads = flat_events[:, model_width:].reshape(events, H, model_width // H)
    scores = (
        jnp.einsum("chd,ehd->che", query_heads, key_heads, preferred_element_type=jnp.float32)
        * score_scale
    )
    weights = (jax.nn.silu(scores) * live_mask[:, None, :]).astype(jnp.bfloat16)
    return (scores, weights, key_heads, value_heads)


def backward_core(
    query_heads, back_att, scores, weights, key_heads, value_heads, live_mask, score_scale
):
    back_w = jnp.einsum("chd,ehd->che", back_att, value_heads, preferred_element_type=jnp.float32)
    back_s = (back_w * live_mask[:, None, :] * silu_slope(scores) * score_scale).astype(
        jnp.bfloat16
    )
    back_query = jnp.einsum("che,ehd->chd", back_s, key_heads, preferred_element_type=jnp.float32)
    key_part = jnp.einsum("che,chd->ehd", back_s, query_heads, preferred_element_type=jnp.float32)
    value_part = jnp.einsum("che,chd->ehd", weights, back_att, preferred_element_type=jnp.float32)
    events = key_part.shape[0]
    joined = jnp.concatenate([key_part.reshape(events, -1), value_part.reshape(events, -1)], axis=1)
    return (back_query, joined.astype(jnp.bfloat16))


def take_columns(table, indices):
    return jnp.take(table, indices, axis=1)


def on_device(
    dense_feat, emb_ids, tables, history_kv, hist_len, cand_request, w_query, w_out, cotangent
):
    tab_dev, emb_width, table_rows = tables.shape
    bag_size = emb_ids.shape[1]
    group_size = emb_ids.shape[2]
    pooled_sum = jnp.zeros((tab_dev, emb_width, group_size), jnp.float32)
    for slot in range(bag_size):
        pooled_sum = pooled_sum + jax.vmap(take_columns)(tables, emb_ids[:, slot, :]).astype(
            jnp.float32
        )
    pooled_rows = pooled_sum.astype(jnp.bfloat16).reshape(tab_dev * emb_width, group_size)
    pooled_cols = lax.all_to_all(pooled_rows, "cand", split_axis=1, concat_axis=0, tiled=True)
    pooled = jnp.transpose(pooled_cols, (1, 0))
    features = jnp.concatenate([pooled, dense_feat], axis=1)
    cand_count, model_width = features.shape
    pooled_width = pooled.shape[1]
    head_dim = model_width // H
    score_scale = 1.0 / math.sqrt(head_dim)
    owned_count, shard_events, kv_width = history_kv.shape
    hist_events = shard_events * lax.axis_size("cand")
    full_query, full_out = (
        lax.all_gather(w_query, ("req", "cand"), axis=0, tiled=True),
        lax.all_gather(w_out, ("req", "cand"), axis=0, tiled=True),
    )
    query_pre = jnp.dot(features, full_query, preferred_element_type=jnp.float32)
    query_heads = jax.nn.silu(query_pre).astype(jnp.bfloat16).reshape(cand_count, H, head_dim)
    full_history = lax.all_gather(history_kv, "cand", axis=1, tiled=True)
    live_mask = event_mask(cand_request, hist_len, hist_events)
    scores, weights, key_heads, value_heads = forward_events(
        query_heads, full_history, live_mask, score_scale
    )
    attended = jnp.einsum("che,ehd->chd", weights, value_heads, preferred_element_type=jnp.float32)
    attended = attended.reshape(cand_count, model_width)
    centered = attended - jnp.mean(attended, axis=1, keepdims=True)
    inverse = lax.rsqrt(jnp.mean(centered * centered, axis=1, keepdims=True) + norm_eps)
    normed = centered * inverse
    normed_b = normed.astype(jnp.bfloat16)
    mixed_out = jnp.dot(normed_b, full_out, preferred_element_type=jnp.float32)
    back_y = lax.dot_general(
        cotangent, full_out, (((1,), (1,)), ((), ())), preferred_element_type=jnp.float32
    )
    cand_out = (mixed_out + features.astype(jnp.float32)).astype(jnp.bfloat16)
    back_att = inverse * (
        back_y
        - jnp.mean(back_y, axis=1, keepdims=True)
        - normed * jnp.mean(back_y * normed, axis=1, keepdims=True)
    )
    back_att = back_att.astype(jnp.bfloat16).reshape(cand_count, H, head_dim)
    back_query, joined = backward_core(
        query_heads, back_att, scores, weights, key_heads, value_heads, live_mask, score_scale
    )
    kv_part = joined.reshape(owned_count, hist_events, kv_width)
    d_kv = lax.psum_scatter(kv_part, "cand", scatter_dimension=1, tiled=True).astype(jnp.float32)
    back_pre = (back_query.reshape(cand_count, model_width) * silu_slope(query_pre)).astype(
        jnp.bfloat16
    )
    back_columns = lax.dot_general(
        back_pre,
        full_query[:pooled_width],
        (((1,), (1,)), ((), ())),
        preferred_element_type=jnp.float32,
    )
    back_pool = (cotangent[:, :pooled_width].astype(jnp.float32) + back_columns).astype(
        jnp.bfloat16
    )
    pool_cols = jnp.transpose(back_pool, (1, 0))
    pool_rows = lax.all_to_all(pool_cols, "cand", split_axis=0, concat_axis=1, tiled=True)
    d_pooled = pool_rows.reshape(tab_dev, emb_width, pool_rows.shape[1])
    return (cand_out, d_kv, d_pooled)


MESH = pl.DeviceIdType.MESH
LOOKUP_DEPTH = 512
LOOKUP_WIDTH = 256


def flip(index, bit):
    return index + bit - 2 * bit * lax.rem(lax.div(index, bit), 2)


def powers(count):
    return [1 << k for k in reversed(range(count.bit_length() - 1))]


class Gather:
    def __init__(self, full, own, rounds, place, sends, recvs):
        self.full, self.own, self.rounds, self.place = full, own, rounds, place
        self.sends, self.recvs, self.rows = sends, recvs, own.shape[0]
        self.count = 1 << len(rounds)

    def device(self, subset):
        req, cand = lax.axis_index("req"), lax.axis_index("cand")
        for step, (axis, bit) in enumerate(self.rounds):
            if subset >> step & 1:
                if axis == "req":
                    req = flip(req, bit)
                else:
                    cand = flip(cand, bit)
        return req, cand

    def block(self, subset):
        first = pl.multiple_of(self.place(*self.device(subset)) * self.rows, self.rows)
        return self.full.at[pl.ds(first, self.rows)]

    def copy(self, subset, arrived):
        step = subset.bit_length() - 1
        sent = subset - (1 << step)
        here = self.block(subset if arrived else sent)
        return pltpu.make_async_remote_copy(
            src_ref=self.own if sent == 0 and not arrived else here,
            dst_ref=here,
            send_sem=self.sends.at[subset],
            recv_sem=self.recvs.at[subset],
            device_id=self.device(1 << step),
            device_id_type=MESH,
        )

    def forward(self, subset):
        if subset:
            self.copy(subset, True).wait_recv()
        for step in range(subset.bit_length(), len(self.rounds)):
            self.copy(subset + (1 << step), False).start()

    def keep_own(self):
        self.block(0)[...] = self.own[...]

    def drain(self):
        for subset in range(1, self.count):
            self.copy(subset, False).wait_send()


def dot_nt(left, right):
    return lax.dot_general(
        left, right, (((1,), (1,)), ((), ())), preferred_element_type=jnp.float32
    )


def dot_tn(left, right):
    return lax.dot_general(
        left, right, (((0,), (0,)), ((), ())), preferred_element_type=jnp.float32
    )


def dot_nn(left, right):
    return jnp.dot(left, right, preferred_element_type=jnp.float32)


def layer_kernel(
    n_req,
    n_cand,
    lens_ref,
    dense_ref,
    ids_ref,
    table_ref,
    hist_ref,
    requests_ref,
    wq_ref,
    wo_ref,
    cot_ref,
    out_ref,
    dkv_ref,
    dpool_ref,
    wq,
    wo,
    hist,
    lookup,
    pool_acc,
    pool_send,
    pool_recv,
    att,
    query,
    back_att,
    scores_s,
    weights_s,
    back_query,
    part,
    part_recv,
    grad_send,
    grad_recv,
    wq_sends,
    wq_recvs,
    wo_sends,
    wo_recvs,
    hist_sends,
    hist_recvs,
    pool_sends,
    pool_recvs,
    part_sends,
    part_recvs,
    grad_sends,
    grad_recvs,
):
    req, cand = lax.axis_index("req"), lax.axis_index("cand")
    cand_count, model_width = cot_ref.shape
    emb_width = table_ref.shape[0]
    head_dim = model_width // H
    owned = lens_ref.shape[0]
    block_events = hist_ref.shape[0]
    events = block_events * n_cand
    shard_events = block_events // owned
    pooled_width = emb_width * n_cand
    score_scale = 1.0 / math.sqrt(head_dim)

    barrier = pltpu.get_barrier_semaphore()
    greeted = [(flip(req, bit), cand) for bit in powers(n_req)]
    greeted += [(req, lax.rem(cand + k, n_cand)) for k in range(1, n_cand)]
    for device in greeted:
        pl.semaphore_signal(barrier, inc=1, device_id=device, device_id_type=MESH)
    pl.semaphore_wait(barrier, len(greeted))

    req_rounds = [("req", bit) for bit in powers(n_req)]
    cand_rounds = [("cand", bit) for bit in powers(n_cand)]
    swapped = cand_rounds[:-1][::-1] + cand_rounds[-1:]

    def linear(r, c):
        return r * n_cand + c

    def in_group(r, c):
        return c

    gq = Gather(wq, wq_ref, req_rounds + cand_rounds, linear, wq_sends, wq_recvs)
    go = Gather(wo, wo_ref, req_rounds + swapped, linear, wo_sends, wo_recvs)
    gh = Gather(hist, hist_ref, cand_rounds, in_group, hist_sends, hist_recvs)
    gq.forward(0)
    gh.forward(0)
    go.forward(0)
    for gather in (gq, gh, go):
        gather.keep_own()

    def exchange(source, target, sends, recvs, rows, k):
        peer = lax.rem(cand + k, n_cand)
        sent = pl.ds(pl.multiple_of(peer * rows, rows), rows)
        mine = pl.ds(pl.multiple_of(cand * rows, rows), rows)
        return pltpu.make_async_remote_copy(
            src_ref=source.at[sent],
            dst_ref=target.at[mine],
            send_sem=sends.at[k],
            recv_sem=recvs.at[k],
            device_id=(req, peer),
            device_id_type=MESH,
        )

    def start_all(*buffers):
        for k in range(1, n_cand):
            exchange(*buffers, k).start()

    def own_rows(source, target, rows):
        mine = pl.ds(pl.multiple_of(cand * rows, rows), rows)
        target[mine] = source[mine]

    def wait_all(*buffers):
        for k in range(1, n_cand):
            exchange(*buffers, k).wait()

    highs = table_ref.shape[1] // LOOKUP_DEPTH
    for high in range(highs):
        lookup[high * emb_width : (high + 1) * emb_width, :] = table_ref[
            :, high * LOOKUP_DEPTH : (high + 1) * LOOKUP_DEPTH
        ]
    pool_acc[...] = jnp.zeros_like(pool_acc)
    chunks = ids_ref.shape[1] // LOOKUP_WIDTH
    steps = chunks * ids_ref.shape[0]

    def look_up(step, carry):
        slot = lax.div(step, chunks)
        columns = pl.ds(
            pl.multiple_of(lax.rem(step, chunks) * LOOKUP_WIDTH, LOOKUP_WIDTH), LOOKUP_WIDTH
        )
        ids = ids_ref[pl.ds(slot, 1), columns]
        low = ids & (LOOKUP_DEPTH - 1)
        high_ids = ids >> (LOOKUP_DEPTH.bit_length() - 1)
        rows = lax.broadcasted_iota(jnp.int32, (LOOKUP_DEPTH, LOOKUP_WIDTH), 0)
        hot = jnp.where(rows == low, 1.0, 0.0).astype(jnp.bfloat16)
        found = dot_nn(lookup[...], hot)
        high_rows = jnp.broadcast_to(high_ids, (emb_width, LOOKUP_WIDTH))
        total = pool_acc[:, columns]
        picked = jnp.zeros_like(total)
        for high in range(highs):
            piece = found[high * emb_width : (high + 1) * emb_width, :]
            picked = picked + jnp.where(high_rows == high, piece, 0.0)
        pool_acc[:, columns] = total + picked
        return carry

    lax.fori_loop(0, steps // 2, look_up, 0)
    for subset in range(1, 4):
        gq.forward(subset)
        go.forward(subset)
    lax.fori_loop(steps // 2, steps, look_up, 0)
    for k in range(n_cand):
        pool_send[k * emb_width : (k + 1) * emb_width, :] = pool_acc[
            :, k * cand_count : (k + 1) * cand_count
        ].astype(jnp.bfloat16)
    pool = (pool_send, pool_recv, pool_sends, pool_recvs, emb_width)
    start_all(*pool)
    own_rows(pool_send, pool_recv, emb_width)
    for subset in range(1, gh.count // 2):
        gh.forward(subset)
    for subset in range(4, gq.count // 2):
        gq.forward(subset)
        go.forward(subset)

    event = lax.broadcasted_iota(jnp.int32, (events, cand_count), 0)
    owner = lax.div(lax.rem(event, block_events), shard_events)
    position = lax.div(event, block_events) * shard_events + lax.rem(event, shard_events)
    limit = jnp.zeros_like(event)
    for index in range(owned):
        limit = jnp.where(owner == index, lens_ref[index], limit)
    alive = (requests_ref[...] == owner) & (position < limit)
    live = jnp.where(alive, 1.0, 0.0).T

    wait_all(*pool)
    pooled = pool_recv[...].astype(jnp.float32).T.astype(jnp.bfloat16)
    for subset in range(gh.count // 2, gh.count):
        gh.forward(subset)
    for subset in range(gq.count // 2, gq.count):
        gq.forward(subset)

    query_pre = dot_nn(pooled, wq[:pooled_width, :]) + dot_nn(
        dense_ref[...], wq[pooled_width:, :]
    )
    gate = jax.nn.sigmoid(query_pre)
    query[...] = (query_pre * gate).astype(jnp.bfloat16)
    slope_pre = gate * (1.0 + query_pre * (1.0 - gate))
    for head in range(H):
        cols = slice(head * head_dim, (head + 1) * head_dim)
        value_cols = slice(model_width + head * head_dim, model_width + (head + 1) * head_dim)
        scores = dot_nt(query[:, cols], hist[:, cols]) * score_scale
        chance = jax.nn.sigmoid(scores)
        weights = (scores * chance * live).astype(jnp.bfloat16)
        weights_s[head] = weights
        scores_s[head] = chance * (1.0 + scores * (1.0 - chance)) * live
        att[:, cols] = dot_nn(weights, hist[:, value_cols])
    attended = att[...]
    centered = attended - jnp.mean(attended, axis=1, keepdims=True)
    inverse = lax.rsqrt(jnp.mean(centered * centered, axis=1, keepdims=True) + norm_eps)
    normed = centered * inverse
    for subset in range(go.count // 2, go.count):
        go.forward(subset)
    back_y = dot_nt(cot_ref[...], wo[...])
    back_att[...] = (
        inverse
        * (
            back_y
            - jnp.mean(back_y, axis=1, keepdims=True)
            - normed * jnp.mean(back_y * normed, axis=1, keepdims=True)
        )
    ).astype(jnp.bfloat16)
    for head in range(H):
        cols = slice(head * head_dim, (head + 1) * head_dim)
        value_cols = slice(model_width + head * head_dim, model_width + (head + 1) * head_dim)
        back_w = dot_nt(back_att[:, cols], hist[:, value_cols])
        back_s = (back_w * scores_s[head] * score_scale).astype(jnp.bfloat16)
        back_query[:, cols] = dot_nn(back_s, hist[:, cols])
        part[:, cols] = dot_tn(back_s, query[:, cols]).astype(jnp.bfloat16)
        part[:, value_cols] = dot_tn(weights_s[head], back_att[:, cols]).astype(jnp.bfloat16)
    parts = (part, part_recv, part_sends, part_recvs, block_events)
    start_all(*parts)
    own_rows(part, part_recv, block_events)
    back_pre = (back_query[...] * slope_pre).astype(jnp.bfloat16)
    back_columns = dot_nt(wq[:pooled_width, :], back_pre)
    direct = cot_ref[:, :pooled_width].astype(jnp.float32).T
    grad_send[...] = (direct + back_columns).astype(jnp.bfloat16)
    grads = (grad_send, grad_recv, grad_sends, grad_recvs, emb_width)
    start_all(*grads)
    own_rows(grad_send, grad_recv, emb_width)

    normed_b = normed.astype(jnp.bfloat16)
    mixed = dot_nn(normed_b, wo[...])
    out_ref[:, :pooled_width] = (mixed[:, :pooled_width] + pooled.astype(jnp.float32)).astype(
        jnp.bfloat16
    )
    out_ref[:, pooled_width:] = (
        mixed[:, pooled_width:] + dense_ref[...].astype(jnp.float32)
    ).astype(jnp.bfloat16)
    wait_all(*grads)
    for k in range(n_cand):
        dpool_ref[:, k * cand_count : (k + 1) * cand_count] = grad_recv[
            k * emb_width : (k + 1) * emb_width, :
        ]
    wait_all(*parts)
    total = part_recv[:block_events, :].astype(jnp.float32)
    for k in range(1, n_cand):
        total = total + part_recv[k * block_events : (k + 1) * block_events, :].astype(jnp.float32)
    dkv_ref[...] = total
    for gather in (gq, gh, go):
        gather.drain()


def one_kernel(
    n_req,
    n_cand,
    dense_feat,
    emb_ids,
    tables,
    history_kv,
    hist_len,
    cand_request,
    w_query,
    w_out,
    cotangent,
):
    cand_count, model_width = cotangent.shape
    owned, shard_events, kv_width = history_kv.shape
    emb_width, table_rows = tables.shape[1:]
    group_size = emb_ids.shape[2]
    block_events = owned * shard_events
    events = block_events * n_cand
    pooled_width = emb_width * n_cand
    bf16, f32 = jnp.bfloat16, jnp.float32
    dma = pltpu.SemaphoreType.DMA
    vmem = pl.BlockSpec(memory_space=pltpu.VMEM)
    scratch = [
        pltpu.VMEM((model_width, model_width), bf16),
        pltpu.VMEM((model_width, model_width), bf16),
        pltpu.VMEM((events, kv_width), bf16),
        pltpu.VMEM((table_rows // LOOKUP_DEPTH * emb_width, LOOKUP_DEPTH), bf16),
        pltpu.VMEM((emb_width, group_size), f32),
        pltpu.VMEM((pooled_width, cand_count), bf16),
        pltpu.VMEM((pooled_width, cand_count), bf16),
        pltpu.VMEM((cand_count, model_width), f32),
        pltpu.VMEM((cand_count, model_width), bf16),
        pltpu.VMEM((cand_count, model_width), bf16),
        pltpu.VMEM((H, cand_count, events), f32),
        pltpu.VMEM((H, cand_count, events), bf16),
        pltpu.VMEM((cand_count, model_width), f32),
        pltpu.VMEM((events, kv_width), bf16),
        pltpu.VMEM((events, kv_width), bf16),
        pltpu.VMEM((pooled_width, cand_count), bf16),
        pltpu.VMEM((pooled_width, cand_count), bf16),
    ]
    scratch += [dma((n_req * n_cand,))] * 4 + [dma((n_cand,))] * 8
    out, d_kv, d_pooled = pl.pallas_call(
        functools.partial(layer_kernel, n_req, n_cand),
        out_shape=(
            jax.ShapeDtypeStruct((cand_count, model_width), bf16),
            jax.ShapeDtypeStruct((block_events, kv_width), f32),
            jax.ShapeDtypeStruct((emb_width, group_size), bf16),
        ),
        in_specs=[pl.BlockSpec(memory_space=pltpu.SMEM)] + [vmem] * 8,
        out_specs=(vmem, vmem, vmem),
        scratch_shapes=scratch,
        compiler_params=pltpu.CompilerParams(
            collective_id=0, has_side_effects=True, vmem_limit_bytes=44 << 20
        ),
    )(
        hist_len,
        dense_feat,
        emb_ids.reshape(emb_ids.shape[1:]),
        tables.reshape(emb_width, table_rows),
        history_kv.reshape(block_events, kv_width),
        cand_request.reshape(1, cand_count),
        w_query,
        w_out,
        cotangent,
    )
    return (
        out,
        d_kv.reshape(history_kv.shape),
        d_pooled.reshape(1, emb_width, group_size),
    )


def pick_plan(n_req, n_cand, *args):
    _, emb_ids, tables, history_kv, _, _, w_query, _, _ = args
    aligned = (
        tables.shape[0] == 1
        and w_query.shape[0] % 16 == 0
        and history_kv.shape[1] % 8 == 0
        and history_kv.shape[0] * history_kv.shape[1] % 16 == 0
        and tables.shape[2] % LOOKUP_DEPTH == 0
        and emb_ids.shape[2] % LOOKUP_WIDTH == 0
    )
    if aligned:
        return one_kernel(n_req, n_cand, *args)
    return on_device(*args)


def solution(mesh):
    plan = functools.partial(pick_plan, mesh.shape["req"], mesh.shape["cand"])
    return jax.shard_map(
        plan,
        mesh=mesh,
        in_specs=(
            P(("req", "cand"), None),
            P("cand", None, "req"),
            P("cand", None, None),
            P("req", "cand", None),
            P("req"),
            P(("req", "cand")),
            P(("req", "cand"), None),
            P(("req", "cand"), None),
            P(("req", "cand"), None),
        ),
        out_specs=(P(("req", "cand"), None), P("req", "cand", None), P("cand", None, "req")),
        check_vma=False,
    )
```

```python
import functools
import math

import jax
import jax.numpy as jnp
from jax import lax
from jax.experimental import pallas as pl
from jax.experimental.pallas import tpu as pltpu
from jax.sharding import PartitionSpec as P

H = 8


norm_eps = 1e-05


def silu_slope(argument):
    sigmoid_value = jax.nn.sigmoid(argument)
    return sigmoid_value * (1.0 + argument * (1.0 - sigmoid_value))


def event_mask(requests, lengths, row_count):
    owned_count = lengths.shape[0]
    positions = jnp.arange(row_count, dtype=jnp.int32)
    in_length = positions[None, :] < lengths[:, None]
    same_request = requests[:, None] == jnp.arange(owned_count, dtype=jnp.int32)[None, :]
    joined_mask = same_request[:, :, None] & in_length[None, :, :]
    return joined_mask.reshape(requests.shape[0], owned_count * row_count).astype(jnp.float32)


def forward_events(query_heads, kv_piece, live_mask, score_scale):
    owned_count, row_count, kv_width = kv_piece.shape
    model_width = kv_width // 2
    events = owned_count * row_count
    flat_events = kv_piece.reshape(events, kv_width)
    key_heads = flat_events[:, :model_width].reshape(events, H, model_width // H)
    value_heads = flat_events[:, model_width:].reshape(events, H, model_width // H)
    scores = (
        jnp.einsum("chd,ehd->che", query_heads, key_heads, preferred_element_type=jnp.float32)
        * score_scale
    )
    weights = (jax.nn.silu(scores) * live_mask[:, None, :]).astype(jnp.bfloat16)
    return (scores, weights, key_heads, value_heads)


def backward_core(
    query_heads, back_att, scores, weights, key_heads, value_heads, live_mask, score_scale
):
    back_w = jnp.einsum("chd,ehd->che", back_att, value_heads, preferred_element_type=jnp.float32)
    back_s = (back_w * live_mask[:, None, :] * silu_slope(scores) * score_scale).astype(
        jnp.bfloat16
    )
    back_query = jnp.einsum("che,ehd->chd", back_s, key_heads, preferred_element_type=jnp.float32)
    key_part = jnp.einsum("che,chd->ehd", back_s, query_heads, preferred_element_type=jnp.float32)
    value_part = jnp.einsum("che,chd->ehd", weights, back_att, preferred_element_type=jnp.float32)
    events = key_part.shape[0]
    joined = jnp.concatenate([key_part.reshape(events, -1), value_part.reshape(events, -1)], axis=1)
    return (back_query, joined.astype(jnp.bfloat16))


def take_columns(table, indices):
    return jnp.take(table, indices, axis=1)


def on_device(
    dense_feat, emb_ids, tables, history_kv, hist_len, cand_request, w_query, w_out, cotangent
):
    tab_dev, emb_width, table_rows = tables.shape
    bag_size = emb_ids.shape[1]
    group_size = emb_ids.shape[2]
    pooled_sum = jnp.zeros((tab_dev, emb_width, group_size), jnp.float32)
    for slot in range(bag_size):
        pooled_sum = pooled_sum + jax.vmap(take_columns)(tables, emb_ids[:, slot, :]).astype(
            jnp.float32
        )
    pooled_rows = pooled_sum.astype(jnp.bfloat16).reshape(tab_dev * emb_width, group_size)
    pooled_cols = lax.all_to_all(pooled_rows, "cand", split_axis=1, concat_axis=0, tiled=True)
    pooled = jnp.transpose(pooled_cols, (1, 0))
    features = jnp.concatenate([pooled, dense_feat], axis=1)
    cand_count, model_width = features.shape
    pooled_width = pooled.shape[1]
    head_dim = model_width // H
    score_scale = 1.0 / math.sqrt(head_dim)
    owned_count, shard_events, kv_width = history_kv.shape
    hist_events = shard_events * lax.axis_size("cand")
    full_query, full_out = (
        lax.all_gather(w_query, ("req", "cand"), axis=0, tiled=True),
        lax.all_gather(w_out, ("req", "cand"), axis=0, tiled=True),
    )
    query_pre = jnp.dot(features, full_query, preferred_element_type=jnp.float32)
    query_heads = jax.nn.silu(query_pre).astype(jnp.bfloat16).reshape(cand_count, H, head_dim)
    full_history = lax.all_gather(history_kv, "cand", axis=1, tiled=True)
    live_mask = event_mask(cand_request, hist_len, hist_events)
    scores, weights, key_heads, value_heads = forward_events(
        query_heads, full_history, live_mask, score_scale
    )
    attended = jnp.einsum("che,ehd->chd", weights, value_heads, preferred_element_type=jnp.float32)
    attended = attended.reshape(cand_count, model_width)
    centered = attended - jnp.mean(attended, axis=1, keepdims=True)
    inverse = lax.rsqrt(jnp.mean(centered * centered, axis=1, keepdims=True) + norm_eps)
    normed = centered * inverse
    normed_b = normed.astype(jnp.bfloat16)
    mixed_out = jnp.dot(normed_b, full_out, preferred_element_type=jnp.float32)
    back_y = lax.dot_general(
        cotangent, full_out, (((1,), (1,)), ((), ())), preferred_element_type=jnp.float32
    )
    cand_out = (mixed_out + features.astype(jnp.float32)).astype(jnp.bfloat16)
    back_att = inverse * (
        back_y
        - jnp.mean(back_y, axis=1, keepdims=True)
        - normed * jnp.mean(back_y * normed, axis=1, keepdims=True)
    )
    back_att = back_att.astype(jnp.bfloat16).reshape(cand_count, H, head_dim)
    back_query, joined = backward_core(
        query_heads, back_att, scores, weights, key_heads, value_heads, live_mask, score_scale
    )
    kv_part = joined.reshape(owned_count, hist_events, kv_width)
    d_kv = lax.psum_scatter(kv_part, "cand", scatter_dimension=1, tiled=True).astype(jnp.float32)
    back_pre = (back_query.reshape(cand_count, model_width) * silu_slope(query_pre)).astype(
        jnp.bfloat16
    )
    back_columns = lax.dot_general(
        back_pre,
        full_query[:pooled_width],
        (((1,), (1,)), ((), ())),
        preferred_element_type=jnp.float32,
    )
    back_pool = (cotangent[:, :pooled_width].astype(jnp.float32) + back_columns).astype(
        jnp.bfloat16
    )
    pool_cols = jnp.transpose(back_pool, (1, 0))
    pool_rows = lax.all_to_all(pool_cols, "cand", split_axis=0, concat_axis=1, tiled=True)
    d_pooled = pool_rows.reshape(tab_dev, emb_width, pool_rows.shape[1])
    return (cand_out, d_kv, d_pooled)


MESH = pl.DeviceIdType.MESH
LOOKUP_DEPTH = 512
LOOKUP_WIDTH = 256


def flip(index, bit):
    return index + bit - 2 * bit * lax.rem(lax.div(index, bit), 2)


def powers(count):
    return [1 << k for k in reversed(range(count.bit_length() - 1))]


class Gather:
    def __init__(self, full, own, rounds, place, sends, recvs, first=0):
        self.full, self.own, self.rounds, self.place = full, own, rounds, place
        self.sends, self.recvs, self.rows = sends, recvs, own.shape[0]
        self.first = first
        self.count = 1 << len(rounds)

    def device(self, subset):
        req, cand = lax.axis_index("req"), lax.axis_index("cand")
        for step, (axis, bit) in enumerate(self.rounds):
            if subset >> step & 1:
                if axis == "req":
                    req = flip(req, bit)
                else:
                    cand = flip(cand, bit)
        return req, cand

    def block(self, subset):
        first = pl.multiple_of(self.place(*self.device(subset)) * self.rows, self.rows)
        return self.full.at[pl.ds(first, self.rows)]

    def copy(self, subset, arrived):
        step = subset.bit_length() - 1
        sent = subset - (1 << step)
        here = self.block(subset if arrived else sent)
        return pltpu.make_async_remote_copy(
            src_ref=self.own if sent == 0 and not arrived else here,
            dst_ref=here,
            send_sem=self.sends.at[self.first + subset],
            recv_sem=self.recvs.at[self.first + subset],
            device_id=self.device(1 << step),
            device_id_type=MESH,
        )

    def forward(self, subset):
        if subset:
            self.copy(subset, True).wait_recv()
        for step in range(subset.bit_length(), len(self.rounds)):
            self.copy(subset + (1 << step), False).start()

    def keep_own(self, sem):
        return pltpu.make_async_copy(self.own, self.block(0), sem)

    def drain(self):
        for subset in range(1, self.count):
            self.copy(subset, False).wait_send()


def dot_nt(left, right):
    return lax.dot_general(
        left, right, (((1,), (1,)), ((), ())), preferred_element_type=jnp.float32
    )


def dot_tn(left, right):
    return lax.dot_general(
        left, right, (((0,), (0,)), ((), ())), preferred_element_type=jnp.float32
    )


def dot_nn(left, right):
    return jnp.dot(left, right, preferred_element_type=jnp.float32)


def layer_kernel(
    n_req,
    n_cand,
    lens_hbm,
    dense_hbm,
    ids_hbm,
    table_hbm,
    hist_ref,
    requests_hbm,
    wq_ref,
    wo_ref,
    cot_hbm,
    out_ref,
    dkv_ref,
    dpool_ref,
    lens_ref,
    dense_ref,
    ids_ref,
    table_ref,
    requests_ref,
    cot_ref,
    wq,
    wo,
    hist,
    lookup,
    pool_acc,
    pool_send,
    pool_recv,
    att,
    query,
    back_att,
    scores_s,
    weights_s,
    back_query,
    part,
    part_recv,
    grad_send,
    grad_recv,
    wq_sends,
    wq_recvs,
    wo_sends,
    wo_recvs,
    hist_sends,
    hist_recvs,
    pool_sends,
    pool_recvs,
    part_sends,
    part_recvs,
    grad_sends,
    grad_recvs,
    load_sems,
):
    req, cand = lax.axis_index("req"), lax.axis_index("cand")
    cand_count, model_width = cot_ref.shape
    emb_width = table_ref.shape[0]
    head_dim = model_width // H
    owned = lens_ref.shape[1]
    block_events = hist_ref.shape[0]
    events = block_events * n_cand
    shard_events = block_events // owned
    pooled_width = emb_width * n_cand
    score_scale = 1.0 / math.sqrt(head_dim)

    loads = [
        pltpu.make_async_copy(source, target, load_sems.at[index])
        for index, (source, target) in enumerate(
            [
                (table_hbm, table_ref),
                (ids_hbm, ids_ref),
                (lens_hbm, lens_ref),
                (requests_hbm, requests_ref),
                (dense_hbm, dense_ref),
                (cot_hbm, cot_ref),
            ]
        )
    ]
    for load in loads:
        load.start()

    barrier = pltpu.get_barrier_semaphore()
    greeted = [(flip(req, bit), cand) for bit in powers(n_req)]
    greeted += [(req, lax.rem(cand + k, n_cand)) for k in range(1, n_cand)]
    for device in greeted:
        pl.semaphore_signal(barrier, inc=1, device_id=device, device_id_type=MESH)
    pl.semaphore_wait(barrier, len(greeted))

    req_rounds = [("req", bit) for bit in powers(n_req)]
    cand_rounds = [("cand", bit) for bit in powers(n_cand)]
    swapped = cand_rounds[:-1][::-1] + cand_rounds[-1:]

    def in_group(r, c):
        return c

    def halves(full, own, sends, recvs):
        rows = own.shape[0] // 2
        gathers = []
        for half, order in enumerate((cand_rounds, swapped)):
            gathers.append(
                Gather(
                    full,
                    own.at[pl.ds(half * rows, rows)],
                    req_rounds + order,
                    lambda r, c, half=half: (r * n_cand + c) * 2 + half,
                    sends,
                    recvs,
                    half * n_req * n_cand,
                )
            )
        return gathers

    gq = halves(wq, wq_ref, wq_sends, wq_recvs)
    go = halves(wo, wo_ref, wo_sends, wo_recvs)
    gh = Gather(hist, hist_ref, cand_rounds, in_group, hist_sends, hist_recvs)
    last = len(req_rounds + cand_rounds) - 1

    def advance(pair, step):
        for subset in range((1 << step) // 2, 1 << step):
            for gather in pair:
                gather.forward(subset)

    advance(gq, 0)
    gh.forward(0)
    loads += [
        gather.keep_own(load_sems.at[len(loads) + index])
        for index, gather in enumerate((*gq, gh, *go))
    ]
    for load in loads[-5:]:
        load.start()
    for load in loads[:2]:
        load.wait()

    def exchange(source, target, sends, recvs, rows, k):
        peer = lax.rem(cand + k, n_cand)
        sent = pl.ds(pl.multiple_of(peer * rows, rows), rows)
        mine = pl.ds(pl.multiple_of(cand * rows, rows), rows)
        return pltpu.make_async_remote_copy(
            src_ref=source.at[sent],
            dst_ref=target.at[mine],
            send_sem=sends.at[k],
            recv_sem=recvs.at[k],
            device_id=(req, peer),
            device_id_type=MESH,
        )

    def start_all(*buffers):
        for k in range(1, n_cand):
            exchange(*buffers, k).start()

    def own_rows(source, target, rows):
        mine = pl.ds(pl.multiple_of(cand * rows, rows), rows)
        target[mine] = source[mine]

    def wait_all(*buffers):
        for k in range(1, n_cand):
            exchange(*buffers, k).wait()

    highs = table_ref.shape[1] // LOOKUP_DEPTH
    for high in range(highs):
        lookup[high * emb_width : (high + 1) * emb_width, :] = table_ref[
            :, high * LOOKUP_DEPTH : (high + 1) * LOOKUP_DEPTH
        ]
    pool_acc[...] = jnp.zeros_like(pool_acc)
    chunks = ids_ref.shape[1] // LOOKUP_WIDTH
    steps = chunks * ids_ref.shape[0]

    def look_up(step, carry):
        slot = lax.div(step, chunks)
        columns = pl.ds(
            pl.multiple_of(lax.rem(step, chunks) * LOOKUP_WIDTH, LOOKUP_WIDTH), LOOKUP_WIDTH
        )
        ids = ids_ref[pl.ds(slot, 1), columns]
        low = ids & (LOOKUP_DEPTH - 1)
        high_ids = ids >> (LOOKUP_DEPTH.bit_length() - 1)
        rows = lax.broadcasted_iota(jnp.int32, (LOOKUP_DEPTH, LOOKUP_WIDTH), 0)
        hot = jnp.where(rows == low, 1.0, 0.0).astype(jnp.bfloat16)
        found = dot_nn(lookup[...], hot)
        high_rows = jnp.broadcast_to(high_ids, (emb_width, LOOKUP_WIDTH))
        total = pool_acc[:, columns]
        picked = jnp.zeros_like(total)
        for high in range(highs):
            piece = found[high * emb_width : (high + 1) * emb_width, :]
            picked = picked + jnp.where(high_rows == high, piece, 0.0)
        pool_acc[:, columns] = total + picked
        return carry

    quarter = steps // 4
    for turn in range(4):
        lax.fori_loop(turn * quarter, (turn + 1) * quarter, look_up, 0)
        if turn + 1 < min(4, last):
            advance(gq, turn + 1)
            advance(go, turn)
    for k in range(n_cand):
        pool_send[k * emb_width : (k + 1) * emb_width, :] = pool_acc[
            :, k * cand_count : (k + 1) * cand_count
        ].astype(jnp.bfloat16)
    pool = (pool_send, pool_recv, pool_sends, pool_recvs, emb_width)
    start_all(*pool)
    own_rows(pool_send, pool_recv, emb_width)
    for subset in range(1, gh.count // 2):
        gh.forward(subset)
    for step in range(min(4, last), last + 1):
        advance(gq, step)
        advance(go, step - 1)

    for load in loads[2:]:
        load.wait()
    event = lax.broadcasted_iota(jnp.int32, (events, cand_count), 0)
    owner = lax.div(lax.rem(event, block_events), shard_events)
    position = lax.div(event, block_events) * shard_events + lax.rem(event, shard_events)
    limit = jnp.zeros_like(event)
    for index in range(owned):
        limit = jnp.where(owner == index, lens_ref[:, index : index + 1], limit)
    alive = (requests_ref[...] == owner) & (position < limit)
    live = jnp.where(alive, 1.0, 0.0).T

    wait_all(*pool)
    pooled = pool_recv[...].astype(jnp.float32).T.astype(jnp.bfloat16)
    for subset in range(gh.count // 2, gh.count):
        gh.forward(subset)
    advance(gq, last + 1)

    query_pre = dot_nn(pooled, wq[:pooled_width, :]) + dot_nn(
        dense_ref[...], wq[pooled_width:, :]
    )
    gate = jax.nn.sigmoid(query_pre)
    query[...] = (query_pre * gate).astype(jnp.bfloat16)
    advance(go, last)
    slope_pre = gate * (1.0 + query_pre * (1.0 - gate))
    for head in range(H):
        cols = slice(head * head_dim, (head + 1) * head_dim)
        value_cols = slice(model_width + head * head_dim, model_width + (head + 1) * head_dim)
        scores = dot_nt(query[:, cols], hist[:, cols]) * score_scale
        chance = jax.nn.sigmoid(scores)
        weights = (scores * chance * live).astype(jnp.bfloat16)
        weights_s[head] = weights
        scores_s[head] = chance * (1.0 + scores * (1.0 - chance)) * live
        att[:, cols] = dot_nn(weights, hist[:, value_cols])
    attended = att[...]
    centered = attended - jnp.mean(attended, axis=1, keepdims=True)
    inverse = lax.rsqrt(jnp.mean(centered * centered, axis=1, keepdims=True) + norm_eps)
    normed = centered * inverse
    advance(go, last + 1)
    back_y = dot_nt(cot_ref[...], wo[...])
    back_att[...] = (
        inverse
        * (
            back_y
            - jnp.mean(back_y, axis=1, keepdims=True)
            - normed * jnp.mean(back_y * normed, axis=1, keepdims=True)
        )
    ).astype(jnp.bfloat16)
    for head in range(H):
        cols = slice(head * head_dim, (head + 1) * head_dim)
        value_cols = slice(model_width + head * head_dim, model_width + (head + 1) * head_dim)
        back_w = dot_nt(back_att[:, cols], hist[:, value_cols])
        back_s = (back_w * scores_s[head] * score_scale).astype(jnp.bfloat16)
        back_query[:, cols] = dot_nn(back_s, hist[:, cols])
        part[:, cols] = dot_tn(back_s, query[:, cols]).astype(jnp.bfloat16)
        part[:, value_cols] = dot_tn(weights_s[head], back_att[:, cols]).astype(jnp.bfloat16)
    parts = (part, part_recv, part_sends, part_recvs, block_events)
    start_all(*parts)
    own_rows(part, part_recv, block_events)
    back_pre = (back_query[...] * slope_pre).astype(jnp.bfloat16)
    back_columns = dot_nt(wq[:pooled_width, :], back_pre)
    direct = cot_ref[:, :pooled_width].astype(jnp.float32).T
    grad_send[...] = (direct + back_columns).astype(jnp.bfloat16)
    grads = (grad_send, grad_recv, grad_sends, grad_recvs, emb_width)
    start_all(*grads)
    own_rows(grad_send, grad_recv, emb_width)

    normed_b = normed.astype(jnp.bfloat16)
    mixed = dot_nn(normed_b, wo[...])
    out_ref[:, :pooled_width] = (mixed[:, :pooled_width] + pooled.astype(jnp.float32)).astype(
        jnp.bfloat16
    )
    out_ref[:, pooled_width:] = (
        mixed[:, pooled_width:] + dense_ref[...].astype(jnp.float32)
    ).astype(jnp.bfloat16)
    wait_all(*grads)
    for k in range(n_cand):
        dpool_ref[:, k * cand_count : (k + 1) * cand_count] = grad_recv[
            k * emb_width : (k + 1) * emb_width, :
        ]
    for gather in (*gq, gh, *go):
        gather.drain()
    wait_all(*parts)
    total = part_recv[:block_events, :].astype(jnp.float32)
    for k in range(1, n_cand):
        total = total + part_recv[k * block_events : (k + 1) * block_events, :].astype(jnp.float32)
    dkv_ref[...] = total


def one_kernel(
    n_req,
    n_cand,
    dense_feat,
    emb_ids,
    tables,
    history_kv,
    hist_len,
    cand_request,
    w_query,
    w_out,
    cotangent,
):
    cand_count, model_width = cotangent.shape
    owned, shard_events, kv_width = history_kv.shape
    emb_width, table_rows = tables.shape[1:]
    group_size = emb_ids.shape[2]
    block_events = owned * shard_events
    events = block_events * n_cand
    pooled_width = emb_width * n_cand
    bf16, f32 = jnp.bfloat16, jnp.float32
    dma = pltpu.SemaphoreType.DMA
    vmem = pl.BlockSpec(memory_space=pltpu.VMEM)
    vmem_like = [
        pltpu.VMEM((1, owned), jnp.int32),
        pltpu.VMEM((cand_count, model_width - pooled_width), bf16),
        pltpu.VMEM(emb_ids.shape[1:], jnp.int32),
        pltpu.VMEM((emb_width, table_rows), bf16),
        pltpu.VMEM((1, cand_count), jnp.int32),
        pltpu.VMEM((cand_count, model_width), bf16),
    ]
    scratch = vmem_like + [
        pltpu.VMEM((model_width, model_width), bf16),
        pltpu.VMEM((model_width, model_width), bf16),
        pltpu.VMEM((events, kv_width), bf16),
        pltpu.VMEM((table_rows // LOOKUP_DEPTH * emb_width, LOOKUP_DEPTH), bf16),
        pltpu.VMEM((emb_width, group_size), f32),
        pltpu.VMEM((pooled_width, cand_count), bf16),
        pltpu.VMEM((pooled_width, cand_count), bf16),
        pltpu.VMEM((cand_count, model_width), f32),
        pltpu.VMEM((cand_count, model_width), bf16),
        pltpu.VMEM((cand_count, model_width), bf16),
        pltpu.VMEM((H, cand_count, events), f32),
        pltpu.VMEM((H, cand_count, events), bf16),
        pltpu.VMEM((cand_count, model_width), f32),
        pltpu.VMEM((events, kv_width), bf16),
        pltpu.VMEM((events, kv_width), bf16),
        pltpu.VMEM((pooled_width, cand_count), bf16),
        pltpu.VMEM((pooled_width, cand_count), bf16),
    ]
    scratch += [dma((2 * n_req * n_cand,))] * 4 + [dma((n_cand,))] * 8 + [dma((11,))]
    out, d_kv, d_pooled = pl.pallas_call(
        functools.partial(layer_kernel, n_req, n_cand),
        out_shape=(
            jax.ShapeDtypeStruct((cand_count, model_width), bf16),
            jax.ShapeDtypeStruct((block_events, kv_width), f32),
            jax.ShapeDtypeStruct((emb_width, group_size), bf16),
        ),
        in_specs=[pl.BlockSpec(memory_space=pltpu.HBM)] * 9,
        out_specs=(vmem, vmem, vmem),
        scratch_shapes=scratch,
        compiler_params=pltpu.CompilerParams(
            collective_id=0, has_side_effects=True, vmem_limit_bytes=63 << 20
        ),
    )(
        hist_len.reshape(1, owned),
        dense_feat,
        emb_ids.reshape(emb_ids.shape[1:]),
        tables.reshape(emb_width, table_rows),
        history_kv.reshape(block_events, kv_width),
        cand_request.reshape(1, cand_count),
        w_query,
        w_out,
        cotangent,
    )
    return (
        out,
        d_kv.reshape(history_kv.shape),
        d_pooled.reshape(1, emb_width, group_size),
    )


def pick_plan(n_req, n_cand, *args):
    _, emb_ids, tables, history_kv, _, _, w_query, _, _ = args
    aligned = (
        tables.shape[0] == 1
        and w_query.shape[0] % 32 == 0
        and history_kv.shape[1] % 8 == 0
        and history_kv.shape[0] * history_kv.shape[1] % 16 == 0
        and tables.shape[2] % LOOKUP_DEPTH == 0
        and emb_ids.shape[1] * emb_ids.shape[2] % (4 * LOOKUP_WIDTH) == 0
        and emb_ids.shape[2] % LOOKUP_WIDTH == 0
    )
    if aligned:
        return one_kernel(n_req, n_cand, *args)
    return on_device(*args)


def solution(mesh):
    plan = functools.partial(pick_plan, mesh.shape["req"], mesh.shape["cand"])
    return jax.shard_map(
        plan,
        mesh=mesh,
        in_specs=(
            P(("req", "cand"), None),
            P("cand", None, "req"),
            P("cand", None, None),
            P("req", "cand", None),
            P("req"),
            P(("req", "cand")),
            P(("req", "cand"), None),
            P(("req", "cand"), None),
            P(("req", "cand"), None),
        ),
        out_specs=(P(("req", "cand"), None), P("req", "cand", None), P("cand", None, "req")),
        check_vma=False,
    )
```

```python
import functools
import math

import jax
import jax.numpy as jnp
from jax import lax
from jax.experimental import pallas as pl
from jax.experimental.pallas import tpu as pltpu
from jax.sharding import PartitionSpec as P

H = 8


norm_eps = 1e-05


def silu_slope(argument):
    sigmoid_value = jax.nn.sigmoid(argument)
    return sigmoid_value * (1.0 + argument * (1.0 - sigmoid_value))


def event_mask(requests, lengths, row_count):
    owned_count = lengths.shape[0]
    positions = jnp.arange(row_count, dtype=jnp.int32)
    in_length = positions[None, :] < lengths[:, None]
    same_request = requests[:, None] == jnp.arange(owned_count, dtype=jnp.int32)[None, :]
    joined_mask = same_request[:, :, None] & in_length[None, :, :]
    return joined_mask.reshape(requests.shape[0], owned_count * row_count).astype(jnp.float32)


def forward_events(query_heads, kv_piece, live_mask, score_scale):
    owned_count, row_count, kv_width = kv_piece.shape
    model_width = kv_width // 2
    events = owned_count * row_count
    flat_events = kv_piece.reshape(events, kv_width)
    key_heads = flat_events[:, :model_width].reshape(events, H, model_width // H)
    value_heads = flat_events[:, model_width:].reshape(events, H, model_width // H)
    scores = (
        jnp.einsum("chd,ehd->che", query_heads, key_heads, preferred_element_type=jnp.float32)
        * score_scale
    )
    weights = (jax.nn.silu(scores) * live_mask[:, None, :]).astype(jnp.bfloat16)
    return (scores, weights, key_heads, value_heads)


def backward_core(
    query_heads, back_att, scores, weights, key_heads, value_heads, live_mask, score_scale
):
    back_w = jnp.einsum("chd,ehd->che", back_att, value_heads, preferred_element_type=jnp.float32)
    back_s = (back_w * live_mask[:, None, :] * silu_slope(scores) * score_scale).astype(
        jnp.bfloat16
    )
    back_query = jnp.einsum("che,ehd->chd", back_s, key_heads, preferred_element_type=jnp.float32)
    key_part = jnp.einsum("che,chd->ehd", back_s, query_heads, preferred_element_type=jnp.float32)
    value_part = jnp.einsum("che,chd->ehd", weights, back_att, preferred_element_type=jnp.float32)
    events = key_part.shape[0]
    joined = jnp.concatenate([key_part.reshape(events, -1), value_part.reshape(events, -1)], axis=1)
    return (back_query, joined.astype(jnp.bfloat16))


def take_columns(table, indices):
    return jnp.take(table, indices, axis=1)


def on_device(
    dense_feat, emb_ids, tables, history_kv, hist_len, cand_request, w_query, w_out, cotangent
):
    tab_dev, emb_width, table_rows = tables.shape
    bag_size = emb_ids.shape[1]
    group_size = emb_ids.shape[2]
    pooled_sum = jnp.zeros((tab_dev, emb_width, group_size), jnp.float32)
    for slot in range(bag_size):
        pooled_sum = pooled_sum + jax.vmap(take_columns)(tables, emb_ids[:, slot, :]).astype(
            jnp.float32
        )
    pooled_rows = pooled_sum.astype(jnp.bfloat16).reshape(tab_dev * emb_width, group_size)
    pooled_cols = lax.all_to_all(pooled_rows, "cand", split_axis=1, concat_axis=0, tiled=True)
    pooled = jnp.transpose(pooled_cols, (1, 0))
    features = jnp.concatenate([pooled, dense_feat], axis=1)
    cand_count, model_width = features.shape
    pooled_width = pooled.shape[1]
    head_dim = model_width // H
    score_scale = 1.0 / math.sqrt(head_dim)
    owned_count, shard_events, kv_width = history_kv.shape
    hist_events = shard_events * lax.axis_size("cand")
    full_query, full_out = (
        lax.all_gather(w_query, ("req", "cand"), axis=0, tiled=True),
        lax.all_gather(w_out, ("req", "cand"), axis=0, tiled=True),
    )
    query_pre = jnp.dot(features, full_query, preferred_element_type=jnp.float32)
    query_heads = jax.nn.silu(query_pre).astype(jnp.bfloat16).reshape(cand_count, H, head_dim)
    full_history = lax.all_gather(history_kv, "cand", axis=1, tiled=True)
    live_mask = event_mask(cand_request, hist_len, hist_events)
    scores, weights, key_heads, value_heads = forward_events(
        query_heads, full_history, live_mask, score_scale
    )
    attended = jnp.einsum("che,ehd->chd", weights, value_heads, preferred_element_type=jnp.float32)
    attended = attended.reshape(cand_count, model_width)
    centered = attended - jnp.mean(attended, axis=1, keepdims=True)
    inverse = lax.rsqrt(jnp.mean(centered * centered, axis=1, keepdims=True) + norm_eps)
    normed = centered * inverse
    normed_b = normed.astype(jnp.bfloat16)
    mixed_out = jnp.dot(normed_b, full_out, preferred_element_type=jnp.float32)
    back_y = lax.dot_general(
        cotangent, full_out, (((1,), (1,)), ((), ())), preferred_element_type=jnp.float32
    )
    cand_out = (mixed_out + features.astype(jnp.float32)).astype(jnp.bfloat16)
    back_att = inverse * (
        back_y
        - jnp.mean(back_y, axis=1, keepdims=True)
        - normed * jnp.mean(back_y * normed, axis=1, keepdims=True)
    )
    back_att = back_att.astype(jnp.bfloat16).reshape(cand_count, H, head_dim)
    back_query, joined = backward_core(
        query_heads, back_att, scores, weights, key_heads, value_heads, live_mask, score_scale
    )
    kv_part = joined.reshape(owned_count, hist_events, kv_width)
    d_kv = lax.psum_scatter(kv_part, "cand", scatter_dimension=1, tiled=True).astype(jnp.float32)
    back_pre = (back_query.reshape(cand_count, model_width) * silu_slope(query_pre)).astype(
        jnp.bfloat16
    )
    back_columns = lax.dot_general(
        back_pre,
        full_query[:pooled_width],
        (((1,), (1,)), ((), ())),
        preferred_element_type=jnp.float32,
    )
    back_pool = (cotangent[:, :pooled_width].astype(jnp.float32) + back_columns).astype(
        jnp.bfloat16
    )
    pool_cols = jnp.transpose(back_pool, (1, 0))
    pool_rows = lax.all_to_all(pool_cols, "cand", split_axis=0, concat_axis=1, tiled=True)
    d_pooled = pool_rows.reshape(tab_dev, emb_width, pool_rows.shape[1])
    return (cand_out, d_kv, d_pooled)


MESH = pl.DeviceIdType.MESH
LOOKUP_DEPTH = 512
LOOKUP_WIDTH = 256


def flip(index, bit):
    return index + bit - 2 * bit * lax.rem(lax.div(index, bit), 2)


def powers(count):
    return [1 << k for k in reversed(range(count.bit_length() - 1))]


class Gather:
    def __init__(self, full, own, rounds, place, sends, recvs, first=0):
        self.full, self.own, self.rounds, self.place = full, own, rounds, place
        self.sends, self.recvs, self.rows = sends, recvs, own.shape[0]
        self.first = first
        self.count = 1 << len(rounds)

    def device(self, subset):
        req, cand = lax.axis_index("req"), lax.axis_index("cand")
        for step, (axis, bit) in enumerate(self.rounds):
            if subset >> step & 1:
                if axis == "req":
                    req = flip(req, bit)
                else:
                    cand = flip(cand, bit)
        return req, cand

    def block(self, subset):
        first = pl.multiple_of(self.place(*self.device(subset)) * self.rows, self.rows)
        return self.full.at[pl.ds(first, self.rows)]

    def copy(self, subset, arrived):
        step = subset.bit_length() - 1
        sent = subset - (1 << step)
        here = self.block(subset if arrived else sent)
        return pltpu.make_async_remote_copy(
            src_ref=self.own if sent == 0 and not arrived else here,
            dst_ref=here,
            send_sem=self.sends.at[self.first + subset],
            recv_sem=self.recvs.at[self.first + subset],
            device_id=self.device(1 << step),
            device_id_type=MESH,
        )

    def forward(self, subset):
        if subset:
            self.copy(subset, True).wait_recv()
        for step in range(subset.bit_length(), len(self.rounds)):
            self.copy(subset + (1 << step), False).start()

    def keep_own(self, sem):
        return pltpu.make_async_copy(self.own, self.block(0), sem)

    def drain(self):
        for subset in range(1, self.count):
            self.copy(subset, False).wait_send()


def dot_nt(left, right):
    return lax.dot_general(
        left, right, (((1,), (1,)), ((), ())), preferred_element_type=jnp.float32
    )


def dot_tn(left, right):
    return lax.dot_general(
        left, right, (((0,), (0,)), ((), ())), preferred_element_type=jnp.float32
    )


def dot_nn(left, right):
    return jnp.dot(left, right, preferred_element_type=jnp.float32)


def layer_kernel(
    n_req,
    n_cand,
    lens_hbm,
    dense_hbm,
    ids_hbm,
    table_hbm,
    hist_ref,
    requests_hbm,
    wq_ref,
    wo_ref,
    cot_hbm,
    out_ref,
    dkv_ref,
    dpool_ref,
    lens_ref,
    dense_ref,
    ids_ref,
    table_ref,
    requests_ref,
    cot_ref,
    wq,
    wo,
    hist,
    lookup,
    pool_acc,
    pool_send,
    pool_recv,
    att,
    query,
    back_att,
    scores_s,
    weights_s,
    back_query,
    part,
    part_recv,
    grad_send,
    grad_recv,
    wq_sends,
    wq_recvs,
    wo_sends,
    wo_recvs,
    hist_sends,
    hist_recvs,
    pool_sends,
    pool_recvs,
    part_sends,
    part_recvs,
    grad_sends,
    grad_recvs,
    load_sems,
):
    req, cand = lax.axis_index("req"), lax.axis_index("cand")
    cand_count, model_width = cot_ref.shape
    emb_width = table_ref.shape[0]
    head_dim = model_width // H
    owned = lens_ref.shape[1]
    block_events = hist_ref.shape[0]
    events = block_events * n_cand
    shard_events = block_events // owned
    pooled_width = emb_width * n_cand
    score_scale = 1.0 / math.sqrt(head_dim)

    loads = [
        pltpu.make_async_copy(source, target, load_sems.at[index])
        for index, (source, target) in enumerate(
            [
                (table_hbm, table_ref),
                (ids_hbm, ids_ref),
                (lens_hbm, lens_ref),
                (requests_hbm, requests_ref),
                (dense_hbm, dense_ref),
                (cot_hbm, cot_ref),
            ]
        )
    ]
    for load in loads:
        load.start()

    barrier = pltpu.get_barrier_semaphore()
    greeted = [(flip(req, bit), cand) for bit in powers(n_req)]
    greeted += [(req, lax.rem(cand + k, n_cand)) for k in range(1, n_cand)]
    for device in greeted:
        pl.semaphore_signal(barrier, inc=1, device_id=device, device_id_type=MESH)
    pl.semaphore_wait(barrier, len(greeted))

    req_rounds = [("req", bit) for bit in powers(n_req)]
    cand_rounds = [("cand", bit) for bit in powers(n_cand)]
    swapped = cand_rounds[:-1][::-1] + cand_rounds[-1:]

    def in_group(r, c):
        return c

    def halves(full, own, sends, recvs, ahead):
        rows = own.shape[0] // 2
        gathers = []
        for half, order in enumerate((cand_rounds, swapped)):
            gathers.append(
                Gather(
                    full,
                    own.at[pl.ds(half * rows, rows)],
                    order[:ahead] + req_rounds + order[ahead:],
                    lambda r, c, half=half: (r * n_cand + c) * 2 + half,
                    sends,
                    recvs,
                    half * n_req * n_cand,
                )
            )
        return gathers

    gq = halves(wq, wq_ref, wq_sends, wq_recvs, 0)
    go = halves(wo, wo_ref, wo_sends, wo_recvs, 1)
    gh = Gather(hist, hist_ref, cand_rounds, in_group, hist_sends, hist_recvs)
    last = len(req_rounds + cand_rounds) - 1

    def advance(pair, step):
        for subset in range((1 << step) // 2, 1 << step):
            for gather in pair:
                gather.forward(subset)

    advance(gq, 0)
    gh.forward(0)
    loads += [
        gather.keep_own(load_sems.at[len(loads) + index])
        for index, gather in enumerate((*gq, gh, *go))
    ]
    for load in loads[-5:]:
        load.start()
    for load in loads[:2]:
        load.wait()

    def exchange(source, target, sends, recvs, rows, k):
        peer = lax.rem(cand + k, n_cand)
        sent = pl.ds(pl.multiple_of(peer * rows, rows), rows)
        mine = pl.ds(pl.multiple_of(cand * rows, rows), rows)
        return pltpu.make_async_remote_copy(
            src_ref=source.at[sent],
            dst_ref=target.at[mine],
            send_sem=sends.at[k],
            recv_sem=recvs.at[k],
            device_id=(req, peer),
            device_id_type=MESH,
        )

    def start_all(*buffers):
        for k in range(1, n_cand):
            exchange(*buffers, k).start()

    def own_rows(source, target, rows):
        mine = pl.ds(pl.multiple_of(cand * rows, rows), rows)
        target[mine] = source[mine]

    def wait_all(*buffers):
        for k in range(1, n_cand):
            exchange(*buffers, k).wait()

    highs = table_ref.shape[1] // LOOKUP_DEPTH
    for high in range(highs):
        lookup[high * emb_width : (high + 1) * emb_width, :] = table_ref[
            :, high * LOOKUP_DEPTH : (high + 1) * LOOKUP_DEPTH
        ]
    pool_acc[...] = jnp.zeros_like(pool_acc)
    chunks = ids_ref.shape[1] // LOOKUP_WIDTH
    steps = chunks * ids_ref.shape[0]

    def look_up(step, carry):
        slot = lax.div(step, chunks)
        columns = pl.ds(
            pl.multiple_of(lax.rem(step, chunks) * LOOKUP_WIDTH, LOOKUP_WIDTH), LOOKUP_WIDTH
        )
        ids = ids_ref[pl.ds(slot, 1), columns]
        low = ids & (LOOKUP_DEPTH - 1)
        high_ids = ids >> (LOOKUP_DEPTH.bit_length() - 1)
        rows = lax.broadcasted_iota(jnp.int32, (LOOKUP_DEPTH, LOOKUP_WIDTH), 0)
        hot = jnp.where(rows == low, 1.0, 0.0).astype(jnp.bfloat16)
        found = dot_nn(lookup[...], hot)
        high_rows = jnp.broadcast_to(high_ids, (emb_width, LOOKUP_WIDTH))
        total = pool_acc[:, columns]
        picked = jnp.zeros_like(total)
        for high in range(highs):
            piece = found[high * emb_width : (high + 1) * emb_width, :]
            picked = picked + jnp.where(high_rows == high, piece, 0.0)
        pool_acc[:, columns] = total + picked
        return carry

    quarter = steps // 4
    for turn in range(4):
        lax.fori_loop(turn * quarter, (turn + 1) * quarter, look_up, 0)
        if turn + 1 < min(4, last):
            advance(gq, turn + 1)
            advance(go, turn)
    for k in range(n_cand):
        pool_send[k * emb_width : (k + 1) * emb_width, :] = pool_acc[
            :, k * cand_count : (k + 1) * cand_count
        ].astype(jnp.bfloat16)
    pool = (pool_send, pool_recv, pool_sends, pool_recvs, emb_width)
    start_all(*pool)
    own_rows(pool_send, pool_recv, emb_width)
    for subset in range(1, gh.count // 2):
        gh.forward(subset)
    for step in range(min(4, last), last + 1):
        advance(gq, step)
        advance(go, step - 1)

    for load in loads[2:]:
        load.wait()
    event = lax.broadcasted_iota(jnp.int32, (events, cand_count), 0)
    owner = lax.div(lax.rem(event, block_events), shard_events)
    position = lax.div(event, block_events) * shard_events + lax.rem(event, shard_events)
    limit = jnp.zeros_like(event)
    for index in range(owned):
        limit = jnp.where(owner == index, lens_ref[:, index : index + 1], limit)
    alive = (requests_ref[...] == owner) & (position < limit)
    live = jnp.where(alive, 1.0, 0.0).T

    wait_all(*pool)
    pooled = pool_recv[...].astype(jnp.float32).T.astype(jnp.bfloat16)
    for subset in range(gh.count // 2, gh.count):
        gh.forward(subset)
    advance(gq, last + 1)

    query_pre = dot_nn(pooled, wq[:pooled_width, :]) + dot_nn(
        dense_ref[...], wq[pooled_width:, :]
    )
    gate = jax.nn.sigmoid(query_pre)
    query[...] = (query_pre * gate).astype(jnp.bfloat16)
    advance(go, last)
    slope_pre = gate * (1.0 + query_pre * (1.0 - gate))
    for head in range(H):
        cols = slice(head * head_dim, (head + 1) * head_dim)
        value_cols = slice(model_width + head * head_dim, model_width + (head + 1) * head_dim)
        scores = dot_nt(query[:, cols], hist[:, cols]) * score_scale
        chance = jax.nn.sigmoid(scores)
        weights = (scores * chance * live).astype(jnp.bfloat16)
        weights_s[head] = weights
        scores_s[head] = chance * (1.0 + scores * (1.0 - chance)) * live
        att[:, cols] = dot_nn(weights, hist[:, value_cols])
    attended = att[...]
    centered = attended - jnp.mean(attended, axis=1, keepdims=True)
    inverse = lax.rsqrt(jnp.mean(centered * centered, axis=1, keepdims=True) + norm_eps)
    normed = centered * inverse
    advance(go, last + 1)
    back_y = dot_nt(cot_ref[...], wo[...])
    back_att[...] = (
        inverse
        * (
            back_y
            - jnp.mean(back_y, axis=1, keepdims=True)
            - normed * jnp.mean(back_y * normed, axis=1, keepdims=True)
        )
    ).astype(jnp.bfloat16)
    for head in range(H):
        cols = slice(head * head_dim, (head + 1) * head_dim)
        value_cols = slice(model_width + head * head_dim, model_width + (head + 1) * head_dim)
        back_w = dot_nt(back_att[:, cols], hist[:, value_cols])
        back_s = (back_w * scores_s[head] * score_scale).astype(jnp.bfloat16)
        back_query[:, cols] = dot_nn(back_s, hist[:, cols])
        part[:, cols] = dot_tn(back_s, query[:, cols]).astype(jnp.bfloat16)
        part[:, value_cols] = dot_tn(weights_s[head], back_att[:, cols]).astype(jnp.bfloat16)
    parts = (part, part_recv, part_sends, part_recvs, block_events)
    start_all(*parts)
    own_rows(part, part_recv, block_events)
    back_pre = (back_query[...] * slope_pre).astype(jnp.bfloat16)
    back_columns = dot_nt(wq[:pooled_width, :], back_pre)
    direct = cot_ref[:, :pooled_width].astype(jnp.float32).T
    grad_send[...] = (direct + back_columns).astype(jnp.bfloat16)
    grads = (grad_send, grad_recv, grad_sends, grad_recvs, emb_width)
    start_all(*grads)
    own_rows(grad_send, grad_recv, emb_width)

    normed_b = normed.astype(jnp.bfloat16)
    mixed = dot_nn(normed_b, wo[...])
    out_ref[:, :pooled_width] = (mixed[:, :pooled_width] + pooled.astype(jnp.float32)).astype(
        jnp.bfloat16
    )
    out_ref[:, pooled_width:] = (
        mixed[:, pooled_width:] + dense_ref[...].astype(jnp.float32)
    ).astype(jnp.bfloat16)
    wait_all(*grads)
    for k in range(n_cand):
        dpool_ref[:, k * cand_count : (k + 1) * cand_count] = grad_recv[
            k * emb_width : (k + 1) * emb_width, :
        ]
    for gather in (*gq, gh, *go):
        gather.drain()
    wait_all(*parts)
    total = part_recv[:block_events, :].astype(jnp.float32)
    for k in range(1, n_cand):
        total = total + part_recv[k * block_events : (k + 1) * block_events, :].astype(jnp.float32)
    dkv_ref[...] = total


def one_kernel(
    n_req,
    n_cand,
    dense_feat,
    emb_ids,
    tables,
    history_kv,
    hist_len,
    cand_request,
    w_query,
    w_out,
    cotangent,
):
    cand_count, model_width = cotangent.shape
    owned, shard_events, kv_width = history_kv.shape
    emb_width, table_rows = tables.shape[1:]
    group_size = emb_ids.shape[2]
    block_events = owned * shard_events
    events = block_events * n_cand
    pooled_width = emb_width * n_cand
    bf16, f32 = jnp.bfloat16, jnp.float32
    dma = pltpu.SemaphoreType.DMA
    vmem = pl.BlockSpec(memory_space=pltpu.VMEM)
    vmem_like = [
        pltpu.VMEM((1, owned), jnp.int32),
        pltpu.VMEM((cand_count, model_width - pooled_width), bf16),
        pltpu.VMEM(emb_ids.shape[1:], jnp.int32),
        pltpu.VMEM((emb_width, table_rows), bf16),
        pltpu.VMEM((1, cand_count), jnp.int32),
        pltpu.VMEM((cand_count, model_width), bf16),
    ]
    scratch = vmem_like + [
        pltpu.VMEM((model_width, model_width), bf16),
        pltpu.VMEM((model_width, model_width), bf16),
        pltpu.VMEM((events, kv_width), bf16),
        pltpu.VMEM((table_rows // LOOKUP_DEPTH * emb_width, LOOKUP_DEPTH), bf16),
        pltpu.VMEM((emb_width, group_size), f32),
        pltpu.VMEM((pooled_width, cand_count), bf16),
        pltpu.VMEM((pooled_width, cand_count), bf16),
        pltpu.VMEM((cand_count, model_width), f32),
        pltpu.VMEM((cand_count, model_width), bf16),
        pltpu.VMEM((cand_count, model_width), bf16),
        pltpu.VMEM((H, cand_count, events), f32),
        pltpu.VMEM((H, cand_count, events), bf16),
        pltpu.VMEM((cand_count, model_width), f32),
        pltpu.VMEM((events, kv_width), bf16),
        pltpu.VMEM((events, kv_width), bf16),
        pltpu.VMEM((pooled_width, cand_count), bf16),
        pltpu.VMEM((pooled_width, cand_count), bf16),
    ]
    scratch += [dma((2 * n_req * n_cand,))] * 4 + [dma((n_cand,))] * 8 + [dma((11,))]
    out, d_kv, d_pooled = pl.pallas_call(
        functools.partial(layer_kernel, n_req, n_cand),
        out_shape=(
            jax.ShapeDtypeStruct((cand_count, model_width), bf16),
            jax.ShapeDtypeStruct((block_events, kv_width), f32),
            jax.ShapeDtypeStruct((emb_width, group_size), bf16),
        ),
        in_specs=[pl.BlockSpec(memory_space=pltpu.HBM)] * 9,
        out_specs=(vmem, vmem, vmem),
        scratch_shapes=scratch,
        compiler_params=pltpu.CompilerParams(
            collective_id=0, has_side_effects=True, vmem_limit_bytes=63 << 20
        ),
    )(
        hist_len.reshape(1, owned),
        dense_feat,
        emb_ids.reshape(emb_ids.shape[1:]),
        tables.reshape(emb_width, table_rows),
        history_kv.reshape(block_events, kv_width),
        cand_request.reshape(1, cand_count),
        w_query,
        w_out,
        cotangent,
    )
    return (
        out,
        d_kv.reshape(history_kv.shape),
        d_pooled.reshape(1, emb_width, group_size),
    )


def pick_plan(n_req, n_cand, *args):
    _, emb_ids, tables, history_kv, _, _, w_query, _, _ = args
    aligned = (
        tables.shape[0] == 1
        and w_query.shape[0] % 32 == 0
        and history_kv.shape[1] % 8 == 0
        and history_kv.shape[0] * history_kv.shape[1] % 16 == 0
        and tables.shape[2] % LOOKUP_DEPTH == 0
        and emb_ids.shape[1] * emb_ids.shape[2] % (4 * LOOKUP_WIDTH) == 0
        and emb_ids.shape[2] % LOOKUP_WIDTH == 0
    )
    if aligned:
        return one_kernel(n_req, n_cand, *args)
    return on_device(*args)


def solution(mesh):
    plan = functools.partial(pick_plan, mesh.shape["req"], mesh.shape["cand"])
    return jax.shard_map(
        plan,
        mesh=mesh,
        in_specs=(
            P(("req", "cand"), None),
            P("cand", None, "req"),
            P("cand", None, None),
            P("req", "cand", None),
            P("req"),
            P(("req", "cand")),
            P(("req", "cand"), None),
            P(("req", "cand"), None),
            P(("req", "cand"), None),
        ),
        out_specs=(P(("req", "cand"), None), P("req", "cand", None), P("cand", None, "req")),
        check_vma=False,
    )
```
